32 devices in a mesh: harm: 4 (over z), pitch: 4 (over x, core), span: 2 (over y).
Axes of the slice: x: 2, y: 2, z: 4, core: 2. Of those that a mesh axis runs over, the one named last changes fastest.
Arguments:
- adjoint_start: float32 [16, 5, 32, 8, 256], P('harm', None, 'pitch', 'span'), may hold values from -6 to 6
- adjoint_source: float32 [16, 5, 32, 8, 256], P('harm', None, 'pitch', 'span'), may hold values from -6 to 6
- coupling: bfloat16 [16, 8, 5, 5, 32, 8, 256], P('harm', None, None, None, 'pitch', 'span'), may hold values from -0.796875 to 0.796875
- diag_inverse: bfloat16 [16, 5, 5, 32, 8, 256], P('harm', None, None, 'pitch', 'span'), may hold values from -0.25 to 0.80078125
- time_weight: float32 [32, 8, 256], P('pitch', 'span'), may hold values from 0.01 to 0.05
- pattern: int32 [32, 8, 8], P('pitch', 'span'), may hold values from 2 to 93, as said below
- face_match: int32 [8, 256], P('span'), may hold values from 0 to 255, each once within a row
- phase_index: int32 [1], replicated, may hold values from 1 to 23
Outputs:
- adjoint: float32 [16, 5, 32, 8, 256], P('harm', None, 'pitch', 'span')
The draws below stay inside these ranges and needn't reach their ends.
Inputs may be any that keep to these rules, and one draw needn't show every extreme that they name: `pattern`: each tile's 8 entries name, in an order drawn for each tile, the tiles one and two places away from it pitchwise and spanwise, as row-major flat indices into its block's grid of (12) x (8) tiles, whose middle holds the block's own tiles. `face_match`: each row is a permutation of 0 to 255.
All inputs are finite; a program needn't handle non-finite values.
Results may differ from the reference program's by a relative error of at most 0.0003.
Values sent between devices are 32-bit elements; how exact they have to be, the bound alone decides.
A program may use at most 128 MiB of HBM per device.

```python
import math
import jax
import jax.numpy as jnp
from jax import lax

NV = 5
LINE = 256
STENCIL = 8
BLADES = 24
SWEEPS = 2
PITCH_TILES = 8
SPAN_TILES = 4
NT = 16
PITCH_ALL = 32
SPAN_ALL = 8
N_PITCH = 4
N_SPAN = 2


def draw_diag_inverse(key, part):
    key_main, key_side = jax.random.split(key)
    shape = (NT, NV, NV, PITCH_ALL, SPAN_ALL, LINE)
    diagonal_part = jax.random.uniform(key_main, shape, jnp.float32, 0.4, 0.8)
    off_part = jax.random.uniform(key_side, shape, jnp.float32, -0.25, 0.25)
    on_diagonal = (jnp.arange(NV)[:, None] == jnp.arange(NV)[None, :])[None, :, :, None, None, None]
    return jnp.where(on_diagonal, diagonal_part, off_part).astype(jnp.bfloat16)


def draw_pattern(key, part):
    row_steps = jnp.array([-1, 1, -2, 2, 0, 0, 0, 0], jnp.int32)
    col_steps = jnp.array([0, 0, 0, 0, -1, 1, -2, 2], jnp.int32)
    scores = jax.random.randint(key, (PITCH_ALL, SPAN_ALL, STENCIL), 0, 1 << 20) * STENCIL
    scores = scores + jnp.arange(STENCIL, dtype=jnp.int32)[None, None, :]
    slot_order = jnp.argsort(scores, axis=-1)
    row_pick = (jnp.arange(PITCH_ALL) % PITCH_TILES)[:, None, None] + 2 + row_steps[slot_order]
    col_pick = (jnp.arange(SPAN_ALL) % SPAN_TILES)[None, :, None] + 2 + col_steps[slot_order]
    return (row_pick * (SPAN_TILES + 4) + col_pick).astype(jnp.int32)


def level_of(own_key, shape, cuts, least, largest):
    loudness = 1.0
    for dim, blocks in cuts:
        steps = jax.random.uniform(jax.random.fold_in(jax.random.fold_in(own_key, 6), dim), (blocks,), jnp.float32, least / len(cuts), largest / len(cuts))
        loudness = loudness * jnp.repeat(jnp.exp(steps), shape[dim] // blocks).reshape((-1,) + (1,) * (len(shape) - 1 - dim))
    return loudness


def bell_draw(key, shape, deviation, bound, cuts=(), kind=jnp.bfloat16):
    drawn = jax.random.normal(key, shape, jnp.float32) * deviation
    if len(cuts) > 0:
        drawn = level_of(key, shape, cuts, -0.22, 0.18) * drawn
    return jnp.clip(drawn, min=-bound, max=bound).astype(kind)


def setup_inputs(seed: int = 0) -> dict:
    keys = jax.random.split(jax.random.key(seed), 9)
    adjoint_start = bell_draw(keys[0], (NT, NV, PITCH_ALL, SPAN_ALL, LINE), 1.0, 6.0, ((0, 4), (2, 4), (3, 2)), jnp.float32)
    adjoint_source = bell_draw(keys[1], (NT, NV, PITCH_ALL, SPAN_ALL, LINE), 1.0, 6.0, ((0, 4), (2, 4), (3, 2)), jnp.float32)
    coupling = bell_draw(keys[2], (NT, STENCIL, NV, NV, PITCH_ALL, SPAN_ALL, LINE), 0.13, 0.796875, ((0, 4), (4, 4), (5, 2)))
    diag_inverse = draw_diag_inverse(jax.random.fold_in(keys[8], 71), 0)
    time_weight = jnp.clip(jnp.exp(math.log(0.05) - 1.609438 * jax.random.uniform(keys[4], (PITCH_ALL, SPAN_ALL, LINE), jnp.float32) ** level_of(keys[4], (PITCH_ALL, SPAN_ALL, LINE), ((0, 4), (1, 2)), -0.2, 0.2)), 0.01, 0.05)
    pattern = draw_pattern(jax.random.fold_in(keys[8], 71), 0)
    face_match = jax.vmap(lambda own: jax.random.permutation(own, LINE))(jax.random.split(keys[6], SPAN_ALL)).reshape((SPAN_ALL, LINE)).astype(jnp.int32)
    phase_index = jax.random.randint(keys[7], (1,), 1, BLADES).astype(jnp.int32)
    return dict(adjoint_start=adjoint_start, adjoint_source=adjoint_source, coupling=coupling, diag_inverse=diag_inverse, time_weight=time_weight, pattern=pattern, face_match=face_match, phase_index=phase_index)


def time_matrix(n_samples):
    row_index = jnp.arange(n_samples)[:, None]
    col_index = jnp.arange(n_samples)[None, :]
    distance = row_index - col_index
    parity = jnp.where(distance % 2 == 0, 1.0, -1.0).astype(jnp.float32)
    angles = math.pi * distance.astype(jnp.float32) / n_samples
    guarded = jnp.where(distance == 0, jnp.float32(1.0), angles)
    values = 0.5 * parity * jnp.cos(guarded) / jnp.sin(guarded)
    return jnp.where(distance == 0, jnp.float32(0.0), values)


def rotation(n_samples, phase_shift):
    row_index = jnp.arange(n_samples)[:, None]
    col_index = jnp.arange(n_samples)[None, :]
    angle_arg = 2.0 * math.pi * (row_index - col_index).astype(jnp.float32) / n_samples + phase_shift
    harmonics = jnp.arange(1, n_samples // 2).astype(jnp.float32)
    summed = 1.0 + 2.0 * jnp.sum(jnp.cos(harmonics[None, None, :] * angle_arg[:, :, None]), axis=2)
    summed = summed + jnp.cos((n_samples // 2) * angle_arg)
    return summed / n_samples


def reference(adjoint_start, adjoint_source, coupling, diag_inverse, time_weight, pattern, face_match, phase_index):
    highest = lax.Precision.HIGHEST
    n_pitch = N_PITCH
    n_span = N_SPAN
    p_tiles = PITCH_TILES
    s_tiles = SPAN_TILES
    derivative = time_matrix(NT)
    phase_shift = 2.0 * math.pi * phase_index[0].astype(jnp.float32) / BLADES
    rot_plus = rotation(NT, phase_shift)
    rot_minus = rotation(NT, -phase_shift)
    inverse = jnp.argsort(face_match, axis=-1).astype(jnp.int32)
    block_pos = jnp.arange(n_pitch)
    at_first = (block_pos == 0)[None, None, :, None, None, None]
    at_last = (block_pos == n_pitch - 1)[None, None, :, None, None, None]
    grid_size = (p_tiles + 4) * (s_tiles + 4)
    tile_index = pattern.reshape(n_pitch, p_tiles, n_span, s_tiles, STENCIL).transpose(0, 2, 1, 3, 4)
    tile_index = tile_index.reshape(n_pitch, n_span, p_tiles * s_tiles * STENCIL).astype(jnp.int32)
    block_id = (jnp.arange(n_pitch)[:, None] * n_span + jnp.arange(n_span)[None, :]).astype(jnp.int32)
    global_index = (block_id[:, :, None] * grid_size + tile_index).reshape(-1).astype(jnp.int32)

    def widen_rows(rows):
        shaped = rows.reshape(NT, NV, n_pitch, 2, n_span, s_tiles, LINE)
        return jnp.pad(shaped, ((0, 0), (0, 0), (0, 0), (0, 0), (0, 0), (2, 2), (0, 0)))

    def per_sample(items):
        jac_part, inv_part, near_part, src_part, time_part = items
        coupled = jnp.einsum("kwvpsc,kwpsc->vpsc", jac_part.astype(jnp.float32), near_part)
        balance = src_part - coupled - time_part
        return jnp.einsum("wvpsc,wpsc->vpsc", inv_part.astype(jnp.float32), balance)

    adjoint_now = adjoint_start
    for sweep_index in range(SWEEPS):
        time_term = time_weight[None, None] * jnp.einsum("mn,mvpsc->nvpsc", derivative, adjoint_now, precision=highest)
        blocks = adjoint_now.reshape(NT, NV, n_pitch, p_tiles, SPAN_ALL, LINE)
        low_rows = blocks[:, :, :, 0:2]
        high_rows = blocks[:, :, :, p_tiles - 2:]
        rot_low = jnp.einsum("nm,mvbrsc->nvbrsc", rot_minus, low_rows, precision=highest)
        rot_high = jnp.einsum("nm,mvbrsc->nvbrsc", rot_plus, high_rows, precision=highest)
        low_perm = jnp.take_along_axis(rot_low, jnp.broadcast_to(inverse, rot_low.shape), axis=5)
        high_perm = jnp.take_along_axis(rot_high, jnp.broadcast_to(face_match, rot_high.shape), axis=5)
        low_send = jnp.where(at_first, low_perm, low_rows)
        high_send = jnp.where(at_last, high_perm, high_rows)
        rows_below = jnp.roll(high_send, 1, axis=2)
        rows_above = jnp.roll(low_send, -1, axis=2)
        columns = blocks.reshape(NT, NV, n_pitch, p_tiles, n_span, s_tiles, LINE)
        zero_cols = jnp.zeros((NT, NV, n_pitch, p_tiles, 1, 2, LINE), jnp.float32)
        lower_cols = jnp.concatenate([zero_cols, columns[:, :, :, :, :-1, s_tiles - 2:]], axis=4)
        upper_cols = jnp.concatenate([columns[:, :, :, :, 1:, 0:2], zero_cols], axis=4)
        middle = jnp.concatenate([lower_cols, columns, upper_cols], axis=5)
        tile_grid = jnp.concatenate([widen_rows(rows_below), middle, widen_rows(rows_above)], axis=3)
        flat_grid = tile_grid.transpose(0, 1, 2, 4, 3, 5, 6).reshape(NT, NV, n_pitch * n_span * grid_size, LINE)
        nearby = jnp.take(flat_grid, global_index, axis=2)
        nearby = nearby.reshape(NT, NV, n_pitch, n_span, p_tiles, s_tiles, STENCIL, LINE)
        nearby = nearby.transpose(0, 6, 1, 2, 4, 3, 5, 7).reshape(NT, STENCIL, NV, PITCH_ALL, SPAN_ALL, LINE)
        adjoint_now = lax.map(per_sample, (coupling, diag_inverse, nearby, adjoint_source, time_term))
    return adjoint_now
```

```python
import functools
import math

import jax
import jax.numpy as jnp
import numpy as np
from jax import lax
from jax.experimental import pallas as pl
from jax.experimental.pallas import tpu as pltpu
from jax.sharding import PartitionSpec as P

BLADES = 24
SWEEPS = 2
MESH = pl.DeviceIdType.MESH
ORDER = (0, 3, 1, 2)


def to_rows(x):
    lead = x.shape[:-3]
    p, s, c = x.shape[-3:]
    x = x.reshape(lead + (p, s, c // 128, 128))
    x = jnp.swapaxes(x, -3, -2)
    return x.reshape(lead + (p * s * c // 128, 128))


def from_rows(x, p, s, c):
    lead = x.shape[:-2]
    x = x.reshape(lead + (p, c // 128, s, 128))
    x = jnp.swapaxes(x, -3, -2)
    return x.reshape(lead + (p, s, c))


def tables(n_samples, phase_index):
    j = np.arange(2 * n_samples) - n_samples
    d = j % n_samples
    safe = np.where(d == 0, 1, d)
    deriv = np.where(d == 0, 0.0, 0.5 * (-1.0) ** d / np.tan(np.pi * safe / n_samples))
    delta = 2.0 * math.pi * phase_index[0].astype(jnp.float32) / BLADES
    angle = jnp.asarray(2.0 * np.pi * d / n_samples, jnp.float32)[None, :]
    angle = angle + delta * jnp.asarray([[1.0], [-1.0]], jnp.float32)
    total = 1.0 + jnp.cos((n_samples // 2) * angle)
    for h in range(1, n_samples // 2):
        total = total + 2.0 * jnp.cos(h * angle)
    return jnp.concatenate([jnp.asarray(deriv, jnp.float32)[None], total / n_samples], axis=0)


def kernel(
    sizes,
    start_ref, source_ref, coupling_ref, diag_ref, weight_ref, pattern_ref, face_ref, tab_ref,
    out_ref,
    adj, src, coup_in, dinv, gath, raw, psend, left, right, coupled, codes, ptmp, onehot, rot2, rot4,
    load_sem, own_sem, zs_sem, zr_sem, rs_sem, rr_sem, ss_sem, sr_sem, ps_sem, pr_sem,
):
    n_loc, n_vars, n_slots, n_chunks, p_count, s_count = sizes
    f32 = jnp.float32
    h = lax.axis_index("harm")
    p = lax.axis_index("pitch")
    q = lax.axis_index("span")
    is_mid = (h == 1) | (h == 2)
    is_end = (h == 0) | (h == 3)
    pair = h + 1 - 2 * lax.rem(h, 2)
    other = 3 - h
    p_next = lax.rem(p + 1, p_count)
    p_prev = lax.rem(p + p_count - 1, p_count)
    has_left = q > 0
    has_right = q < s_count - 1

    loads = [
        pltpu.make_async_copy(start_ref, adj.at[0, :, :, pl.ds(16, 16 * n_chunks)], load_sem.at[0]),
        pltpu.make_async_copy(source_ref, src, load_sem.at[1]),
        pltpu.make_async_copy(diag_ref, dinv, load_sem.at[2]),
    ] + [
        pltpu.make_async_copy(coupling_ref.at[n], coup_in.at[n], load_sem.at[3 + n])
        for n in range(n_loc)
    ]
    for load in loads:
        load.start()

    barrier = pltpu.get_barrier_semaphore()

    def greet(dh, dp, dq):
        pl.semaphore_signal(barrier, inc=1, device_id=(dh, dp, dq), device_id_type=MESH)

    for step in range(1, 4):
        greet(lax.rem(h + step, 4), p, q)
    for dp in (p_next, p_prev):
        greet(h, dp, q)
        greet(pair, dp, q)

    @pl.when(has_left)
    def _():
        greet(h, p, q - 1)

    @pl.when(has_right)
    def _():
        greet(h, p, q + 1)

    pl.semaphore_wait(barrier, 7 + has_left.astype(jnp.int32) + has_right.astype(jnp.int32))

    def rows(c):
        return pl.ds(16 + 16 * c, 16)

    def remote(src_view, dst_view, send, recv, device):
        return pltpu.make_async_remote_copy(
            src_ref=src_view, dst_ref=dst_view, send_sem=send, recv_sem=recv,
            device_id=device, device_id_type=MESH,
        )

    def z_copy(s, c, slot, target):
        return remote(
            adj.at[s, :, :, rows(c)], gath.at[s, c, pl.ds(n_loc * h, n_loc)],
            zs_sem.at[s, c, slot], zr_sem.at[s, c, h], (target, p, q),
        )

    def raw_copy(s, c):
        return remote(
            psend.at[s, c], raw.at[s, c], rs_sem.at[s, c], rr_sem.at[s, c], (pair, p, q)
        )

    def span_copy(s, c, side):
        buf = right if side == 0 else left
        return remote(
            adj.at[s, :, :, rows(c)], buf.at[s, c], ss_sem.at[s, c, side], sr_sem.at[s, c, side],
            (h, p, q - 1 if side == 0 else q + 1),
        )

    def pitch_copy(s, side, src_view, slot, dh):
        dst = adj.at[s, :, :, pl.ds(16 + 16 * n_chunks, 16) if side == 0 else pl.ds(0, 16)]
        return remote(
            src_view, dst, ps_sem.at[s, side, slot], pr_sem.at[s, side],
            (dh, p_prev if side == 0 else p_next, q),
        )

    def plain_pitch(s, side):
        return pitch_copy(s, side, adj.at[s, :, :, rows(0 if side == 0 else n_chunks - 1)], 0, h)

    def rotated(side):
        return p == (0 if side == 0 else p_count - 1)

    def start_sends(s, c):
        @pl.when(is_end)
        def _():
            z_copy(s, c, 0, pair).start()
            z_copy(s, c, 1, 3 - pair).start()

        @pl.when(is_mid)
        def _():
            z_copy(s, c, 0, other).start()

        @pl.when(has_left)
        def _():
            span_copy(s, c, 0).start()

        @pl.when(has_right)
        def _():
            span_copy(s, c, 1).start()

        for side, edge in ((0, 0), (1, n_chunks - 1)):
            if c == edge:
                @pl.when(jnp.logical_not(rotated(side)))
                def _():
                    plain_pitch(s, side).start()

    loads[0].wait()
    for c in ORDER:
        start_sends(0, c)

    @pl.when(jnp.logical_not(has_left))
    def _():
        left[...] = jnp.zeros_like(left)

    @pl.when(jnp.logical_not(has_right))
    def _():
        right[...] = jnp.zeros_like(right)

    for pt in range(2 * n_chunks):
        val = pattern_ref[pt]
        col = lax.broadcasted_iota(jnp.int32, val.shape, 0)
        diff = val - ((pt + 2) * 8 + col + 2)
        code = jnp.zeros_like(diff)
        for number, step in enumerate((-16, -8, 8, 16, -2, -1, 1, 2)):
            code = jnp.where(diff == step, number, code)
        ptmp[pl.ds(8 * pt, 4), :] = code
        ptmp[pl.ds(8 * pt + 4, 4), :] = code
    for k in range(n_slots):
        codes[k] = jnp.broadcast_to(ptmp[:, k : k + 1], codes.shape[1:])

    @pl.when(is_mid & (rotated(0) | rotated(1)))
    def _():
        for sp in range(4):
            match = jnp.broadcast_to(face_ref[sp : sp + 1, :], (256, 256))
            cell = lax.broadcasted_iota(jnp.int32, (256, 256), 0)
            onehot[sp] = jnp.where(match == cell, 1.0, 0.0).astype(jnp.bfloat16)

    sub = lax.rem(lax.broadcasted_iota(jnp.int32, (16, 128), 0), 4)

    def halves(x, shift):
        return jnp.concatenate(
            [pltpu.roll(x[0:8], shift % 8, 0), pltpu.roll(x[8:16], shift % 8, 0)], axis=0
        )

    def span_step(x, lf, rt, step):
        if step < 0:
            return jnp.where(
                sub < -step, halves(lf, -step - 4), halves(x, -step)
            )
        return jnp.where(sub >= 4 - step, halves(rt, 4 - step), halves(x, -step))

    def couple(s, chunk_list):
        count = len(chunk_list)

        def one(i, carry):
            n = lax.rem(i, n_loc)
            c = jnp.int32(chunk_list[0])
            if count > 1:
                c = c + lax.div(i, n_loc) * (chunk_list[1] - chunk_list[0])
            at = pl.multiple_of(16 * c, 16)

            def over_w(w, acc):
                own = adj[s, n, w, pl.ds(at + 16, 16), :]
                lf = left[s, c, n, w]
                rt = right[s, c, n, w]
                cand = [
                    adj[s, n, w, pl.ds(at, 16), :],
                    adj[s, n, w, pl.ds(pl.multiple_of(at + 8, 8), 16), :],
                    adj[s, n, w, pl.ds(pl.multiple_of(at + 24, 8), 16), :],
                    adj[s, n, w, pl.ds(at + 32, 16), :],
                ] + [span_step(own, lf, rt, step) for step in (-2, -1, 1, 2)]
                acc = list(acc)
                for k in range(n_slots):
                    code = codes[k, pl.ds(at, 16), :]
                    m0 = (code & 1) != 0
                    m1 = (code & 2) != 0
                    m2 = code >= 4
                    pairs = [jnp.where(m0, cand[2 * i + 1], cand[2 * i]) for i in range(4)]
                    near = jnp.where(
                        m2, jnp.where(m1, pairs[3], pairs[2]), jnp.where(m1, pairs[1], pairs[0])
                    )
                    for v in range(n_vars):
                        acc[v] = acc[v] + coup_in[n, k, w, v, pl.ds(at, 16), :].astype(f32) * near
                return tuple(acc)

            acc = lax.fori_loop(
                0, n_vars, over_w, tuple(jnp.zeros((16, 128), f32) for _ in range(n_vars))
            )
            for v in range(n_vars):
                coupled[n, v, pl.ds(at, 16), :] = acc[v]
            return carry

        lax.fori_loop(0, n_loc * count, one, 0)

    def mix(s, c, row, group, store):
        first = 4 * n_loc - n_loc * group
        coef = {j: tab_ref[row, first + j] for j in range(1 - n_loc, 4 * n_loc)}

        def over_v(v, carry):
            x = [gath[s, c, m, v] for m in range(4 * n_loc)]
            for i in range(n_loc):
                acc = coef[-i] * x[0]
                for m in range(1, 4 * n_loc):
                    acc = acc + coef[m - i] * x[m]
                store(i, v, acc)
            return carry

        lax.fori_loop(0, n_vars, over_v, 0)

    def turn(s, side):
        c = 0 if side == 0 else n_chunks - 1
        block = n_loc * n_vars * 16
        for which, group in ((0, h), (1, pair)):
            def put(i, v, value, which=which):
                at = pl.multiple_of(which * block + (i * n_vars + v) * 16, 16)
                rot2[pl.ds(at, 16), :] = value

            mix(s, c, 1 + side, group, put)
        count = 2 * block // 8
        for sp in range(4):
            x = jnp.concatenate(
                [rot2[pl.ds(cb * 4 + sp, count, stride=8), :] for cb in range(2)], axis=1
            )
            total = jnp.zeros((count, 256), f32)
            for _ in range(3):
                part = x.astype(jnp.bfloat16)
                x = x - part.astype(f32)
                dims = (((1,), (1,)), ((), ())) if side == 0 else (((1,), (0,)), ((), ()))
                total = total + lax.dot_general(
                    part, onehot[sp], dims, preferred_element_type=f32
                )
            for cb in range(2):
                rot2[pl.ds(cb * 4 + sp, count, stride=8), :] = total[:, 128 * cb : 128 * cb + 128]
        for which in range(2):
            for i in range(n_loc):
                for v in range(n_vars):
                    at = which * block + (i * n_vars + v) * 16
                    rot4[s, which, i, v] = rot2[pl.ds(at, 16), :]
        pitch_copy(s, side, rot4.at[s, 0], 0, h).start()
        pitch_copy(s, side, rot4.at[s, 1], 1, pair).start()

    def times(s, c):
        @pl.when(is_mid)
        def _():
            own = pltpu.make_async_copy(
                adj.at[s, :, :, rows(c)], gath.at[s, c, pl.ds(n_loc * h, n_loc)], own_sem
            )
            own.start()
            own.wait()
            for dh in (pair, other, 3 - pair):
                remote(
                    adj.at[s, :, :, rows(c)], gath.at[s, c, pl.ds(n_loc * dh, n_loc)],
                    zs_sem.at[s, c, 0], zr_sem.at[s, c, dh], (dh, p, q),
                ).wait_recv()

            def put_pair(i, v, value):
                psend[s, c, i, v] = value

            def put_own(i, v, value):
                raw[s, c, i, v] = value

            mix(s, c, 0, pair, put_pair)
            raw_copy(s, c).start()
            for side, edge in ((0, 0), (1, n_chunks - 1)):
                if c == edge:
                    @pl.when(rotated(side))
                    def _():
                        turn(s, side)
            mix(s, c, 0, h, put_own)

    def finish(s, c):
        @pl.when(is_end)
        def _():
            raw_copy(s, c).wait_recv()

        def one(n, carry):
            weight = weight_ref[pl.ds(16 * c, 16), :]
            acc = [jnp.zeros((16, 128), f32) for _ in range(n_vars)]
            for w in range(n_vars):
                balance = (
                    src[n, w, pl.ds(16 * c, 16), :]
                    - coupled[n, w, pl.ds(16 * c, 16), :]
                    - weight * raw[s, c, n, w]
                )
                for v in range(n_vars):
                    acc[v] = acc[v] + dinv[n, w, v, pl.ds(16 * c, 16), :].astype(f32) * balance
            for v in range(n_vars):
                if s + 1 < SWEEPS:
                    adj[s + 1, n, v, rows(c), :] = acc[v]
                else:
                    out_ref[n, v, pl.ds(16 * c, 16), :] = acc[v]
            return carry

        lax.fori_loop(0, n_loc, one, 0)
        if s + 1 < SWEEPS:
            start_sends(s + 1, c)

    def wait_span(s, c):
        @pl.when(has_right)
        def _():
            span_copy(s, c, 0).wait_recv()

        @pl.when(has_left)
        def _():
            span_copy(s, c, 1).wait_recv()

    for load in loads[1:]:
        load.wait()
    for s in range(SWEEPS):
        if s > 0:
            times(s, 0)
            times(s, n_chunks - 1)
        for c in ORDER[2:]:
            wait_span(s, c)
        couple(s, ORDER[2:])
        if s == 0:
            times(s, 0)
            times(s, n_chunks - 1)
        for c in ORDER[:2]:
            wait_span(s, c)
        for side in range(2):
            plain_pitch(s, side).wait_recv()
        couple(s, ORDER[:2])
        finish(s, ORDER[0])
        finish(s, ORDER[1])
        for c in ORDER[2:]:
            times(s, c)
            finish(s, c)

    for s in range(SWEEPS):
        for c in range(n_chunks):
            @pl.when(is_end)
            def _():
                z_copy(s, c, 0, pair).wait_send()
                z_copy(s, c, 1, 3 - pair).wait_send()

            @pl.when(is_mid)
            def _():
                z_copy(s, c, 0, other).wait_send()
                raw_copy(s, c).wait_send()

            @pl.when(has_left)
            def _():
                span_copy(s, c, 0).wait_send()

            @pl.when(has_right)
            def _():
                span_copy(s, c, 1).wait_send()

        for side in range(2):
            @pl.when(jnp.logical_not(rotated(side)))
            def _():
                plain_pitch(s, side).wait_send()

            @pl.when(rotated(side) & is_mid)
            def _():
                pitch_copy(s, side, rot4.at[s, 0], 0, h).wait_send()
                pitch_copy(s, side, rot4.at[s, 1], 1, pair).wait_send()


def local(
    adjoint_start, adjoint_source, coupling, diag_inverse, time_weight, pattern, face_match, phase_index
):
    n_loc, n_vars, p_tiles, s_tiles, line = adjoint_start.shape
    n_slots = pattern.shape[2]
    h_count = lax.axis_size("harm")
    p_count = lax.axis_size("pitch")
    s_count = lax.axis_size("span")
    assert h_count == 4 and s_tiles * line == 1024 and n_slots == 8 and p_count > 2
    n_rows = p_tiles * 8
    n_chunks = p_tiles // 2
    sizes = (n_loc, n_vars, n_slots, n_chunks, p_count, s_count)
    f32, bf16 = jnp.float32, jnp.bfloat16
    hbm = pl.BlockSpec(memory_space=pl.ANY)
    vmem = pl.BlockSpec(memory_space=pltpu.VMEM)
    smem = pl.BlockSpec(memory_space=pltpu.SMEM)
    dma = pltpu.SemaphoreType.DMA
    part = (n_loc, n_vars, 16, 128)
    out = pl.pallas_call(
        functools.partial(kernel, sizes),
        out_shape=jax.ShapeDtypeStruct((n_loc, n_vars, n_rows, 128), f32),
        in_specs=[hbm, hbm, hbm, hbm, vmem, vmem, vmem, smem],
        out_specs=vmem,
        scratch_shapes=[
            pltpu.VMEM((SWEEPS, n_loc, n_vars, n_rows + 32, 128), f32),
            pltpu.VMEM((n_loc, n_vars, n_rows, 128), f32),
            pltpu.VMEM((n_loc, n_slots, n_vars, n_vars, n_rows, 128), bf16),
            pltpu.VMEM((n_loc, n_vars, n_vars, n_rows, 128), bf16),
            pltpu.VMEM((SWEEPS, n_chunks, 4 * n_loc, n_vars, 16, 128), f32),
            pltpu.VMEM((SWEEPS, n_chunks) + part, f32),
            pltpu.VMEM((SWEEPS, n_chunks) + part, f32),
            pltpu.VMEM((SWEEPS, n_chunks) + part, f32),
            pltpu.VMEM((SWEEPS, n_chunks) + part, f32),
            pltpu.VMEM((n_loc, n_vars, n_rows, 128), f32),
            pltpu.VMEM((n_slots, n_rows, 128), jnp.int32),
            pltpu.VMEM((n_rows, n_slots), jnp.int32),
            pltpu.VMEM((4, 256, 256), bf16),
            pltpu.VMEM((2 * n_loc * n_vars * 16, 128), f32),
            pltpu.VMEM((SWEEPS, 2) + part, f32),
            dma((3 + n_loc,)),
            dma,
            dma((SWEEPS, n_chunks, 2)),
            dma((SWEEPS, n_chunks, 4)),
            dma((SWEEPS, n_chunks)),
            dma((SWEEPS, n_chunks)),
            dma((SWEEPS, n_chunks, 2)),
            dma((SWEEPS, n_chunks, 2)),
            dma((SWEEPS, 2, 2)),
            dma((SWEEPS, 2)),
        ],
        compiler_params=pltpu.CompilerParams(
            collective_id=0, has_side_effects=True, vmem_limit_bytes=48 * 1024 * 1024
        ),
        cost_estimate=pl.CostEstimate(flops=40_000_000, bytes_accessed=18_000_000, transcendentals=0),
    )(
        to_rows(adjoint_start),
        to_rows(adjoint_source),
        to_rows(coupling),
        to_rows(diag_inverse),
        to_rows(time_weight),
        pattern,
        face_match,
        tables(n_loc * h_count, phase_index),
    )
    return from_rows(out, p_tiles, s_tiles, line)


def solution(mesh):
    placed = (
        P("harm", None, "pitch", "span", None),
        P("harm", None, "pitch", "span", None),
        P("harm", None, None, None, "pitch", "span", None),
        P("harm", None, None, "pitch", "span", None),
        P("pitch", "span", None),
        P("pitch", "span", None),
        P("span", None),
        P(),
    )
    return jax.shard_map(
        local,
        mesh=mesh,
        in_specs=placed,
        out_specs=P("harm", None, "pitch", "span", None),
        check_vma=False,
    )
```

```python
import functools
import math

import jax
import jax.numpy as jnp
import numpy as np
from jax import lax
from jax.experimental import pallas as pl
from jax.experimental.pallas import tpu as pltpu
from jax.sharding import PartitionSpec as P

BLADES = 24
SWEEPS = 2
MESH = pl.DeviceIdType.MESH
ORDER = (0, 3, 1, 2)


def to_rows(x):
    lead = x.shape[:-3]
    p, s, c = x.shape[-3:]
    x = x.reshape(lead + (p, s, c // 128, 128))
    x = jnp.swapaxes(x, -3, -2)
    return x.reshape(lead + (p * s * c // 128, 128))


def from_rows(x, p, s, c):
    lead = x.shape[:-2]
    x = x.reshape(lead + (p, c // 128, s, 128))
    x = jnp.swapaxes(x, -3, -2)
    return x.reshape(lead + (p, s, c))


def derivative_values(n_samples):
    d = np.arange(n_samples)
    safe = np.where(d == 0, 1, d)
    values = np.where(d == 0, 0.0, 0.5 * (-1.0) ** d / np.tan(np.pi * safe / n_samples))
    return [float(v) for v in values]


def kernel(
    sizes,
    start_ref, source_ref, coupling_ref, diag_ref, weight_hbm, pattern_hbm, face_hbm, phase_ref,
    out_ref,
    adj, src, coup_in, dinv, gath, raw, psend, left, right, coupled, codes, ptmp, onehot, rot2, rot4,
    weight_ref, pattern_ref, face_ref, deriv, vtmp, rtab,
    load_sem, own_sem, zs_sem, zr_sem, rs_sem, rr_sem, ss_sem, sr_sem, ps_sem, pr_sem,
):
    n_loc, n_vars, n_slots, n_chunks, p_count, s_count = sizes
    f32 = jnp.float32
    h = lax.axis_index("harm")
    p = lax.axis_index("pitch")
    q = lax.axis_index("span")
    is_mid = (h == 1) | (h == 2)
    is_end = (h == 0) | (h == 3)
    pair = h + 1 - 2 * lax.rem(h, 2)
    other = 3 - h
    p_next = lax.rem(p + 1, p_count)
    p_prev = lax.rem(p + p_count - 1, p_count)
    has_left = q > 0
    has_right = q < s_count - 1

    loads = [
        pltpu.make_async_copy(start_ref, adj.at[0, :, :, pl.ds(16, 16 * n_chunks)], load_sem.at[0]),
        pltpu.make_async_copy(source_ref, src, load_sem.at[1]),
        pltpu.make_async_copy(diag_ref, dinv, load_sem.at[2]),
        pltpu.make_async_copy(weight_hbm, weight_ref, load_sem.at[3]),
        pltpu.make_async_copy(pattern_hbm, pattern_ref, load_sem.at[4]),
        pltpu.make_async_copy(face_hbm, face_ref, load_sem.at[5]),
    ] + [
        pltpu.make_async_copy(coupling_ref.at[n], coup_in.at[n], load_sem.at[6 + n])
        for n in range(n_loc)
    ]
    for load in loads:
        load.start()

    barrier = pltpu.get_barrier_semaphore()

    def greet(dh, dp, dq):
        pl.semaphore_signal(barrier, inc=1, device_id=(dh, dp, dq), device_id_type=MESH)

    for step in range(1, 4):
        greet(lax.rem(h + step, 4), p, q)
    for dp in (p_next, p_prev):
        greet(h, dp, q)
        greet(pair, dp, q)

    @pl.when(has_left)
    def _():
        greet(h, p, q - 1)

    @pl.when(has_right)
    def _():
        greet(h, p, q + 1)

    pl.semaphore_wait(barrier, 7 + has_left.astype(jnp.int32) + has_right.astype(jnp.int32))

    def rows(c):
        return pl.ds(16 + 16 * c, 16)

    def remote(src_view, dst_view, send, recv, device):
        return pltpu.make_async_remote_copy(
            src_ref=src_view, dst_ref=dst_view, send_sem=send, recv_sem=recv,
            device_id=device, device_id_type=MESH,
        )

    def chunk(s, c, v=slice(None)):
        return adj.at[s, :, v, rows(c)]

    def z_copy(s, c, v, slot, target):
        return remote(
            chunk(s, c, v), gath.at[s, c, pl.ds(n_loc * h, n_loc), v],
            zs_sem.at[s, c, v, slot], zr_sem.at[s, c, v, h], (target, p, q),
        )

    def raw_copy(s, c, v):
        return remote(
            psend.at[s, c, :, v], raw.at[s, c, :, v], rs_sem.at[s, c, v], rr_sem.at[s, c, v],
            (pair, p, q),
        )

    def each_v(body):
        def step(v, carry):
            body(v)
            return carry

        lax.fori_loop(0, n_vars, step, 0)

    def span_copy(s, c, side):
        buf = right if side == 0 else left
        return remote(
            chunk(s, c), buf.at[s, c], ss_sem.at[s, c, side], sr_sem.at[s, c, side],
            (h, p, q - 1 if side == 0 else q + 1),
        )

    def pitch_copy(s, side, src_view, slot, dh):
        dst = adj.at[s, :, :, pl.ds(16 + 16 * n_chunks, 16) if side == 0 else pl.ds(0, 16)]
        return remote(
            src_view, dst, ps_sem.at[s, side, slot], pr_sem.at[s, side],
            (dh, p_prev if side == 0 else p_next, q),
        )

    def plain_pitch(s, side):
        return pitch_copy(s, side, chunk(s, 0 if side == 0 else n_chunks - 1), 0, h)

    def rotated(side):
        return p == (0 if side == 0 else p_count - 1)

    def start_z(s, c):
        @pl.when(is_end)
        def _():
            def send(v):
                z_copy(s, c, v, 0, 3 - pair).start()
                z_copy(s, c, v, 1, pair).start()

            each_v(send)

        @pl.when(is_mid)
        def _():
            each_v(lambda v: z_copy(s, c, v, 0, other).start())

    def wait_z(s, c):
        @pl.when(is_end)
        def _():
            def wait(v):
                z_copy(s, c, v, 0, 3 - pair).wait_send()
                z_copy(s, c, v, 1, pair).wait_send()

            each_v(wait)

        @pl.when(is_mid)
        def _():
            each_v(lambda v: z_copy(s, c, v, 0, other).wait_send())

    def start_sends(s, c):

        @pl.when(has_left)
        def _():
            span_copy(s, c, 0).start()

        @pl.when(has_right)
        def _():
            span_copy(s, c, 1).start()

        for side, edge in ((0, 0), (1, n_chunks - 1)):
            if c == edge:
                @pl.when(jnp.logical_not(rotated(side)))
                def _():
                    plain_pitch(s, side).start()

    loads[0].wait()
    for c in ORDER:
        start_z(0, c)
    for c in ORDER:
        start_sends(0, c)
    for load in loads[1:6]:
        load.wait()

    for j, value in enumerate(2 * derivative_values(4 * n_loc)):
        deriv[j] = jnp.float32(value)

    @pl.when(is_mid & (rotated(0) | rotated(1)))
    def _():
        n_all = 4 * n_loc
        delta = jnp.broadcast_to(phase_ref[0], (8, 128)).astype(f32) * (2.0 * math.pi / BLADES)
        d = lax.rem(lax.broadcasted_iota(jnp.int32, (8, 128), 1), n_all).astype(f32)
        angle = d * (2.0 * math.pi / n_all) + delta
        total = 1.0 + jnp.cos((n_all // 2) * angle)
        for m in range(1, n_all // 2):
            total = total + 2.0 * jnp.cos(m * angle)
        vtmp[...] = total / n_all
        for j in range(2 * n_all):
            rtab[j] = jnp.broadcast_to(vtmp[:, j % n_all : j % n_all + 1], (8, 128))

    @pl.when(jnp.logical_not(has_left))
    def _():
        left[...] = jnp.zeros_like(left)

    @pl.when(jnp.logical_not(has_right))
    def _():
        right[...] = jnp.zeros_like(right)

    for pt in range(2 * n_chunks):
        val = pattern_ref[pt]
        col = lax.broadcasted_iota(jnp.int32, val.shape, 0)
        diff = val - ((pt + 2) * 8 + col + 2)
        code = jnp.zeros_like(diff)
        for number, step in enumerate((-16, -8, 8, 16, -2, -1, 1, 2)):
            code = jnp.where(diff == step, number, code)
        ptmp[pl.ds(8 * pt, 4), :] = code
        ptmp[pl.ds(8 * pt + 4, 4), :] = code
    for k in range(n_slots):
        codes[k] = jnp.broadcast_to(ptmp[:, k : k + 1], codes.shape[1:])

    @pl.when(is_mid & (rotated(0) | rotated(1)))
    def _():
        for sp in range(4):
            match = jnp.broadcast_to(face_ref[sp : sp + 1, :], (256, 256))
            cell = lax.broadcasted_iota(jnp.int32, (256, 256), 0)
            onehot[sp] = jnp.where(match == cell, 1.0, 0.0).astype(jnp.bfloat16)

    sub = lax.rem(lax.broadcasted_iota(jnp.int32, (16, 128), 0), 4)

    def halves(x, shift):
        return jnp.concatenate(
            [pltpu.roll(x[0:8], shift % 8, 0), pltpu.roll(x[8:16], shift % 8, 0)], axis=0
        )

    def span_step(x, lf, rt, step):
        if step < 0:
            return jnp.where(
                sub < -step, halves(lf, -step - 4), halves(x, -step)
            )
        return jnp.where(sub >= 4 - step, halves(rt, 4 - step), halves(x, -step))

    def couple(s, chunk_list):
        count = len(chunk_list)

        def one(i, carry):
            n = lax.rem(i, n_loc)
            c = jnp.int32(chunk_list[0])
            if count > 1:
                c = c + lax.div(i, n_loc) * (chunk_list[1] - chunk_list[0])
            at = pl.multiple_of(16 * c, 16)

            def over_w(w, acc):
                own = adj[s, n, w, pl.ds(at + 16, 16), :]
                lf = left[s, c, n, w]
                rt = right[s, c, n, w]
                cand = [
                    adj[s, n, w, pl.ds(at, 16), :],
                    adj[s, n, w, pl.ds(pl.multiple_of(at + 8, 8), 16), :],
                    adj[s, n, w, pl.ds(pl.multiple_of(at + 24, 8), 16), :],
                    adj[s, n, w, pl.ds(at + 32, 16), :],
                ] + [span_step(own, lf, rt, step) for step in (-2, -1, 1, 2)]
                acc = list(acc)
                for k in range(n_slots):
                    code = codes[k, pl.ds(at, 16), :]
                    m0 = (code & 1) != 0
                    m1 = (code & 2) != 0
                    m2 = code >= 4
                    pairs = [jnp.where(m0, cand[2 * i + 1], cand[2 * i]) for i in range(4)]
                    near = jnp.where(
                        m2, jnp.where(m1, pairs[3], pairs[2]), jnp.where(m1, pairs[1], pairs[0])
                    )
                    for v in range(n_vars):
                        acc[v] = acc[v] + coup_in[n, k, w, v, pl.ds(at, 16), :].astype(f32) * near
                return tuple(acc)

            acc = lax.fori_loop(
                0, n_vars, over_w, tuple(jnp.zeros((16, 128), f32) for _ in range(n_vars))
            )
            for v in range(n_vars):
                coupled[n, v, pl.ds(at, 16), :] = acc[v]
            return carry

        lax.fori_loop(0, n_loc * count, one, 0)

    def mix(s, c, v, group, coef, store):
        first = 4 * n_loc - n_loc * group
        values = {j: coef(first, j) for j in range(1 - n_loc, 4 * n_loc)}
        x = [gath[s, c, m, v] for m in range(4 * n_loc)]
        for i in range(n_loc):
            acc = values[-i] * x[0]
            for m in range(1, 4 * n_loc):
                acc = acc + values[m - i] * x[m]
            store(i, v, acc)

    def time_coef(first, j):
        return deriv[first + j]

    def low_coef(first, j):
        t = rtab[first + j]
        return jnp.concatenate([t, t], axis=0)

    def high_coef(first, j):
        t = rtab[8 * n_loc - first - j]
        return jnp.concatenate([t, t], axis=0)

    def turn(s, side):
        c = 0 if side == 0 else n_chunks - 1
        block = n_loc * n_vars * 16
        for which, group in ((0, h), (1, pair)):
            def put(i, v, value, which=which):
                at = pl.multiple_of(which * block + (i * n_vars + v) * 16, 16)
                rot2[pl.ds(at, 16), :] = value

            coef = low_coef if side == 0 else high_coef
            each_v(lambda v, put=put, group=group: mix(s, c, v, group, coef, put))
        count = 2 * block // 8
        for sp in range(4):
            x = jnp.concatenate(
                [rot2[pl.ds(cb * 4 + sp, count, stride=8), :] for cb in range(2)], axis=1
            )
            total = jnp.zeros((count, 256), f32)
            for _ in range(3):
                part = x.astype(jnp.bfloat16)
                x = x - part.astype(f32)
                dims = (((1,), (1,)), ((), ())) if side == 0 else (((1,), (0,)), ((), ()))
                total = total + lax.dot_general(
                    part, onehot[sp], dims, preferred_element_type=f32
                )
            for cb in range(2):
                rot2[pl.ds(cb * 4 + sp, count, stride=8), :] = total[:, 128 * cb : 128 * cb + 128]
        for which in range(2):
            for i in range(n_loc):
                for v in range(n_vars):
                    at = which * block + (i * n_vars + v) * 16
                    rot4[s, which, i, v] = rot2[pl.ds(at, 16), :]
        pitch_copy(s, side, rot4.at[s, 0], 0, h).start()
        pitch_copy(s, side, rot4.at[s, 1], 1, pair).start()

    def times(s, c):
        @pl.when(is_mid)
        def _():
            own = pltpu.make_async_copy(
                chunk(s, c), gath.at[s, c, pl.ds(n_loc * h, n_loc)], own_sem
            )
            own.start()
            own.wait()

            def put_pair(i, v, value):
                psend[s, c, i, v] = value

            def put_own(i, v, value):
                raw[s, c, i, v] = value

            def relay(v):
                for dh in (pair, other, 3 - pair):
                    remote(
                        chunk(s, c, v), gath.at[s, c, pl.ds(n_loc * dh, n_loc), v],
                        zs_sem.at[s, c, v, 0], zr_sem.at[s, c, v, dh], (dh, p, q),
                    ).wait_recv()
                mix(s, c, v, pair, time_coef, put_pair)
                raw_copy(s, c, v).start()

            each_v(relay)
            for side, edge in ((0, 0), (1, n_chunks - 1)):
                if c == edge:
                    @pl.when(rotated(side))
                    def _():
                        turn(s, side)
            each_v(lambda v: mix(s, c, v, h, time_coef, put_own))

    def finish(s, c):
        @pl.when(is_end)
        def _():
            each_v(lambda v: raw_copy(s, c, v).wait_recv())

        def one(n, carry):
            weight = weight_ref[pl.ds(16 * c, 16), :]
            acc = [jnp.zeros((16, 128), f32) for _ in range(n_vars)]
            for w in range(n_vars):
                balance = (
                    src[n, w, pl.ds(16 * c, 16), :]
                    - coupled[n, w, pl.ds(16 * c, 16), :]
                    - weight * raw[s, c, n, w]
                )
                for v in range(n_vars):
                    acc[v] = acc[v] + dinv[n, w, v, pl.ds(16 * c, 16), :].astype(f32) * balance
            for v in range(n_vars):
                if s + 1 < SWEEPS:
                    adj[s + 1, n, v, rows(c), :] = acc[v]
                else:
                    out_ref[n, v, pl.ds(16 * c, 16), :] = acc[v]
            return carry

        lax.fori_loop(0, n_loc, one, 0)
        if s + 1 < SWEEPS:
            start_z(s + 1, c)
            start_sends(s + 1, c)

    def wait_span(s, c):
        @pl.when(has_right)
        def _():
            span_copy(s, c, 0).wait_recv()

        @pl.when(has_left)
        def _():
            span_copy(s, c, 1).wait_recv()

    for load in loads[6:]:
        load.wait()
    for s in range(SWEEPS):
        if s > 0:
            times(s, 0)
            times(s, n_chunks - 1)
        for c in ORDER[2:]:
            wait_span(s, c)
        couple(s, ORDER[2:])
        if s == 0:
            times(s, 0)
            times(s, n_chunks - 1)
        for c in ORDER[:2]:
            wait_span(s, c)
        for side in range(2):
            plain_pitch(s, side).wait_recv()
        couple(s, ORDER[:2])
        finish(s, ORDER[0])
        finish(s, ORDER[1])
        for c in ORDER[2:]:
            times(s, c)
            finish(s, c)

    for s in range(SWEEPS):
        for c in range(n_chunks):
            wait_z(s, c)

            @pl.when(is_mid)
            def _():
                each_v(lambda v: raw_copy(s, c, v).wait_send())

            @pl.when(has_left)
            def _():
                span_copy(s, c, 0).wait_send()

            @pl.when(has_right)
            def _():
                span_copy(s, c, 1).wait_send()

        for side in range(2):
            @pl.when(jnp.logical_not(rotated(side)))
            def _():
                plain_pitch(s, side).wait_send()

            @pl.when(rotated(side) & is_mid)
            def _():
                pitch_copy(s, side, rot4.at[s, 0], 0, h).wait_send()
                pitch_copy(s, side, rot4.at[s, 1], 1, pair).wait_send()


def local(
    adjoint_start, adjoint_source, coupling, diag_inverse, time_weight, pattern, face_match, phase_index
):
    n_loc, n_vars, p_tiles, s_tiles, line = adjoint_start.shape
    n_slots = pattern.shape[2]
    h_count = lax.axis_size("harm")
    p_count = lax.axis_size("pitch")
    s_count = lax.axis_size("span")
    assert h_count == 4 and s_tiles * line == 1024 and n_slots == 8 and p_count > 2
    n_rows = p_tiles * 8
    n_chunks = p_tiles // 2
    sizes = (n_loc, n_vars, n_slots, n_chunks, p_count, s_count)
    f32, bf16 = jnp.float32, jnp.bfloat16
    hbm = pl.BlockSpec(memory_space=pl.ANY)
    vmem = pl.BlockSpec(memory_space=pltpu.VMEM)
    dma = pltpu.SemaphoreType.DMA
    part = (n_loc, n_vars, 16, 128)
    out = pl.pallas_call(
        functools.partial(kernel, sizes),
        out_shape=jax.ShapeDtypeStruct((n_loc, n_vars, n_rows, 128), f32),
        in_specs=[hbm] * 7 + [pl.BlockSpec(memory_space=pltpu.SMEM)],
        out_specs=vmem,
        scratch_shapes=[
            pltpu.VMEM((SWEEPS, n_loc, n_vars, n_rows + 32, 128), f32),
            pltpu.VMEM((n_loc, n_vars, n_rows, 128), f32),
            pltpu.VMEM((n_loc, n_slots, n_vars, n_vars, n_rows, 128), bf16),
            pltpu.VMEM((n_loc, n_vars, n_vars, n_rows, 128), bf16),
            pltpu.VMEM((SWEEPS, n_chunks, 4 * n_loc, n_vars, 16, 128), f32),
            pltpu.VMEM((SWEEPS, n_chunks) + part, f32),
            pltpu.VMEM((SWEEPS, n_chunks) + part, f32),
            pltpu.VMEM((SWEEPS, n_chunks) + part, f32),
            pltpu.VMEM((SWEEPS, n_chunks) + part, f32),
            pltpu.VMEM((n_loc, n_vars, n_rows, 128), f32),
            pltpu.VMEM((n_slots, n_rows, 128), jnp.int32),
            pltpu.VMEM((n_rows, n_slots), jnp.int32),
            pltpu.VMEM((4, 256, 256), bf16),
            pltpu.VMEM((2 * n_loc * n_vars * 16, 128), f32),
            pltpu.VMEM((SWEEPS, 2) + part, f32),
            pltpu.VMEM((n_rows, 128), f32),
            pltpu.VMEM(pattern.shape, jnp.int32),
            pltpu.VMEM(face_match.shape, jnp.int32),
            pltpu.SMEM((8 * n_loc,), f32),
            pltpu.VMEM((8, 128), f32),
            pltpu.VMEM((8 * n_loc, 8, 128), f32),
            dma((6 + n_loc,)),
            dma,
            dma((SWEEPS, n_chunks, n_vars, 2)),
            dma((SWEEPS, n_chunks, n_vars, 4)),
            dma((SWEEPS, n_chunks, n_vars)),
            dma((SWEEPS, n_chunks, n_vars)),
            dma((SWEEPS, n_chunks, 2)),
            dma((SWEEPS, n_chunks, 2)),
            dma((SWEEPS, 2, 2)),
            dma((SWEEPS, 2)),
        ],
        compiler_params=pltpu.CompilerParams(
            collective_id=0, has_side_effects=True, vmem_limit_bytes=60 * 1024 * 1024
        ),
        cost_estimate=pl.CostEstimate(flops=40_000_000, bytes_accessed=18_000_000, transcendentals=0),
    )(
        to_rows(adjoint_start),
        to_rows(adjoint_source),
        to_rows(coupling),
        to_rows(diag_inverse),
        to_rows(time_weight),
        pattern,
        face_match,
        phase_index,
    )
    return from_rows(out, p_tiles, s_tiles, line)


def solution(mesh):
    placed = (
        P("harm", None, "pitch", "span", None),
        P("harm", None, "pitch", "span", None),
        P("harm", None, None, None, "pitch", "span", None),
        P("harm", None, None, "pitch", "span", None),
        P("pitch", "span", None),
        P("pitch", "span", None),
        P("span", None),
        P(),
    )
    return jax.shard_map(
        local,
        mesh=mesh,
        in_specs=placed,
        out_specs=P("harm", None, "pitch", "span", None),
        check_vma=False,
    )
```
